768 devices in a mesh: dp: 48 (over x, z), tensor: 16 (over y, core).
Axes of the slice: x: 4, y: 8, z: 12, core: 2. Of those that a mesh axis runs over, the one named last changes fastest.
Arguments:
- query_rows: bfloat16 [12288, 6144], P('dp', 'tensor'), may hold values from -128 to 128
- key_rows: bfloat16 [12288, 6144], P('dp', 'tensor'), may hold values from -5 to 5
- value_rows: bfloat16 [12288, 6144], P('dp', 'tensor'), may hold values from -5 to 5
- out_grad: bfloat16 [12288, 6144], P('dp', 'tensor'), may hold values from -5 to 5
- w_query: bfloat16 [3072, 6144], P(None, 'tensor'), may hold values from -0.375 to 0.375
- w_key: bfloat16 [3072, 6144], P(None, 'tensor'), may hold values from -0.375 to 0.375
- w_value: bfloat16 [3072, 6144], P(None, 'tensor'), may hold values from -0.375 to 0.375
- row_image: int32 [12288], P('dp'), may hold values from 0 to 191, as said below
Outputs:
- input_grad: bfloat16 [12288, 3072], P('dp', 'tensor')
The draws below stay inside these ranges and needn't reach their ends.
Inputs may be any that keep to these rules, and one draw needn't show every extreme that they name: `row_image`: image numbers fall into groups d * 4 to d * 4 + 3, one for each index d of dp. In each aligned block of 256 rows at most 13 rows carry numbers of any one group; one group has exactly 13 rows in every block.
All inputs are finite; a program needn't handle non-finite values.
Results may differ from the reference program's by a relative error of at most 0.015.
Values may be sent and summed in bfloat16 or wider, within the bound.
A program may use at most 64 MiB of HBM per device.

```python
import jax
import jax.numpy as jnp
from jax import lax

D = 3072
HEADS = 48
HEAD = 128
TOK_DEV = 256
IMG_DEV = 4
CAP = 13
TOKENS = 12288
N_DP = 48


def routing(key):
    key = jax.random.fold_in(key, 11)
    slot_count = N_DP * CAP
    favour = jax.random.randint(jax.random.fold_in(key, 1), (N_DP,), 0, 4) * 64
    chosen = jax.random.randint(jax.random.fold_in(key, 2), (), 0, N_DP)
    group_of_slot = jnp.arange(slot_count, dtype=jnp.int32) // CAP
    jitter = jax.random.randint(jax.random.fold_in(key, 3), (N_DP, slot_count), 0, 256)
    scores = favour[group_of_slot][None, :] + jitter + jnp.where(group_of_slot == chosen, 1024, 0)[None, :]
    scores = scores * slot_count + jnp.arange(slot_count, dtype=jnp.int32)[None, :]
    ignored, picked = lax.top_k(scores, TOK_DEV)
    ordering = jax.random.randint(jax.random.fold_in(key, 4), (N_DP, TOK_DEV), 0, 1 << 16) * TOK_DEV
    ordering = ordering + jnp.arange(TOK_DEV, dtype=jnp.int32)[None, :]
    shuffle = jnp.argsort(ordering, axis=1)
    picked = jnp.take_along_axis(picked, shuffle, axis=1)
    target = picked // CAP
    within = jax.random.randint(jax.random.fold_in(key, 5), (N_DP, TOK_DEV), 0, IMG_DEV)
    return (target * IMG_DEV + within).reshape(TOKENS).astype(jnp.int32)


def drawn(key):
    stream = jax.random.fold_in(key, 23)
    drawn_q = jnp.clip(jax.random.normal(jax.random.fold_in(stream, 1), (TOKENS, HEADS, HEAD)), -5.0, 5.0)
    drawn_k = jnp.clip(jax.random.normal(jax.random.fold_in(stream, 2), (TOKENS, HEADS, HEAD)), -5.0, 5.0)
    queries = drawn_q
    keys_out = drawn_k
    return (queries.reshape(TOKENS, HEADS * HEAD), keys_out.reshape(TOKENS, HEADS * HEAD))


def draw_row_image(key, part):
    return routing(key)


def draw_query_rows(key, part):
    return drawn(key)[0].astype(jnp.bfloat16)


def draw_key_rows(key, part):
    return drawn(key)[1].astype(jnp.bfloat16)


def block_levels(own_key, extent, pieces, smallest, top_value):
    def one(dim, blocks):
        draws = jax.random.uniform(jax.random.fold_in(jax.random.fold_in(own_key, 6), dim), (blocks,), jnp.float32, smallest / len(pieces), top_value / len(pieces))
        return jnp.repeat(jnp.exp(draws), extent[dim] // blocks).reshape((-1,) + (1,) * (len(extent) - dim - 1))

    loudness = one(*pieces[0])
    for cut in pieces[1:]:
        loudness = loudness * one(*cut)
    return loudness


def centred(own_key, dims, deviation, limit, split=(), kind=jnp.bfloat16):
    values = deviation * jax.random.normal(own_key, dims, jnp.float32)
    if split:
        values = values * block_levels(own_key, dims, split, -0.22, 0.18)
    return jnp.clip(values, -limit, limit).astype(kind)


def setup_inputs(seed: int = 0) -> dict:
    seeds = jax.random.split(jax.random.key(seed), 9)
    query_rows = draw_query_rows(jax.random.fold_in(seeds[8], 71), 0)
    key_rows = draw_key_rows(jax.random.fold_in(seeds[8], 71), 0)
    value_rows = centred(seeds[2], (TOKENS, HEADS * HEAD), 1.0, 5.0, ((0, 48), (1, 16)))
    out_grad = centred(seeds[3], (TOKENS, HEADS * HEAD), 1.0, 5.0, ((0, 48), (1, 16)))
    w_query = centred(seeds[4], (D, HEADS * HEAD), (3 * HEADS * HEAD * IMG_DEV // TOK_DEV) ** -0.5, 0.375, ((1, 16),))
    w_key = centred(seeds[5], (D, HEADS * HEAD), (3 * HEADS * HEAD * IMG_DEV // TOK_DEV) ** -0.5, 0.375, ((1, 16),))
    w_value = centred(seeds[6], (D, HEADS * HEAD), (3 * HEADS * HEAD * IMG_DEV // TOK_DEV) ** -0.5, 0.375, ((1, 16),))
    row_image = draw_row_image(jax.random.fold_in(seeds[8], 71), 0)
    return dict(query_rows=query_rows, key_rows=key_rows, value_rows=value_rows, out_grad=out_grad, w_query=w_query, w_key=w_key, w_value=w_value, row_image=row_image)


def slot_places(row_image):
    target = (row_image // IMG_DEV).astype(jnp.int32)
    onehot = (target[:, None] == jnp.arange(N_DP, dtype=jnp.int32)[None, :]).astype(jnp.int32)
    counted = jnp.cumsum(onehot.reshape(N_DP, TOK_DEV, N_DP), axis=1).astype(jnp.int32).reshape(TOKENS, N_DP)
    position = jnp.sum((counted - 1) * onehot, axis=1).astype(jnp.int32)
    source = jnp.arange(TOKENS, dtype=jnp.int32) // TOK_DEV
    return (target * (N_DP * CAP) + source * CAP + position).astype(jnp.int32)


def attend_back(queries, keys_in, values_in, grad_out, images):
    scale = HEAD ** -0.5
    queries32 = queries.astype(jnp.float32)
    keys32 = keys_in.astype(jnp.float32)
    values32 = values_in.astype(jnp.float32)
    grad32 = grad_out.astype(jnp.float32)
    scores = jnp.einsum("qhe,khe->hqk", queries32, keys32) * scale
    allowed = (images[:, None] == images[None, :])[None, :, :]
    scores = jnp.where(allowed, scores, -1e30)
    highest = jnp.max(scores, axis=2, keepdims=True)
    raised = jnp.where(allowed, jnp.exp(scores - highest), 0.0)
    attention = raised / jnp.sum(raised, axis=2, keepdims=True)
    attention_low = attention.astype(jnp.bfloat16)
    grad_value = jnp.einsum("hqk,qhe->khe", attention_low.astype(jnp.float32), grad32).astype(jnp.bfloat16)
    grad_prob = jnp.einsum("qhe,khe->hqk", grad32, values32)
    row_total = jnp.sum(attention * grad_prob, axis=2, keepdims=True)
    dscore = (attention * (grad_prob - row_total) * scale).astype(jnp.bfloat16).astype(jnp.float32)
    grad_query = jnp.einsum("hqk,khe->qhe", dscore, keys32).astype(jnp.bfloat16)
    grad_key = jnp.einsum("hqk,qhe->khe", dscore, queries32).astype(jnp.bfloat16)
    return grad_query, grad_key, grad_value


def reference(query_rows, key_rows, value_rows, out_grad, w_query, w_key, w_value, row_image):
    placed = slot_places(row_image)
    slot_total = N_DP * N_DP * CAP

    def spread(rows_in):
        empty = jnp.zeros((slot_total, HEADS * HEAD), rows_in.dtype)
        return empty.at[placed].set(rows_in).reshape(N_DP, N_DP * CAP, HEADS, HEAD)

    images = jnp.full((slot_total,), -1, jnp.int32).at[placed].set(row_image).reshape(N_DP, N_DP * CAP)

    def receiver(group):
        return attend_back(group[0], group[1], group[2], group[3], group[4])

    grads = lax.map(receiver, (spread(query_rows), spread(key_rows), spread(value_rows), spread(out_grad), images))

    def restore(grad):
        return grad.reshape(slot_total, HEADS * HEAD)[placed]

    grad_query, grad_key, grad_value = restore(grads[0]), restore(grads[1]), restore(grads[2])
    summed = jnp.dot(grad_query, w_query.T, preferred_element_type=jnp.float32)
    summed = summed + jnp.dot(grad_key, w_key.T, preferred_element_type=jnp.float32)
    summed = summed + jnp.dot(grad_value, w_value.T, preferred_element_type=jnp.float32)
    return summed.astype(jnp.bfloat16)
```

```python
import functools

import jax
import jax.numpy as jnp
from jax import lax
from jax.experimental import pallas as pl
from jax.experimental.pallas import tpu as pltpu
from jax.sharding import PartitionSpec as P

HEAD = 128
IMG_DEV = 4
CAP = 13
PAD = 16
TOGETHER = 6
WINDOW = 32
BLOCK_ROWS = 160
CODE_ROW = 156
GROUP_ROWS = 80
MESH = pl.DeviceIdType.MESH
F32 = jnp.float32
BF16 = jnp.bfloat16


def iota(shape, dim):
    return lax.broadcasted_iota(jnp.int32, shape, dim)


def dot(a, b, contract=((1,), (0,))):
    return lax.dot_general(a, b, (contract, ((), ())), preferred_element_type=F32)


def kernel(
    sizes,
    image_row,
    image_col,
    query,
    key,
    value,
    grad,
    w_query,
    w_key,
    w_value,
    out,
    codes,
    position,
    send,
    recv,
    blocks,
    mask_row,
    mask_col,
    grads,
    weights,
    own,
    sib_send,
    sib_recv,
    ring_send,
    ring_recv,
    back_send,
    back_recv,
    last_send,
    last_recv,
    send_sem,
    recv_sem,
    weight_sem,
    sib_send_sem,
    sib_recv_sem,
    ring_send_sem,
    ring_recv_sem,
    back_send_sem,
    back_recv_sem,
    last_sem,
):
    n_dp, n_y = sizes
    tokens = query.shape[0]
    cols = query.shape[1]
    heads = cols // HEAD
    n_blocks = 4 * heads
    n_groups = n_dp // TOGETHER
    slots = n_groups * GROUP_ROWS
    chains = n_groups // 2
    upward = chains // 2
    chip_cols = out.shape[1] * 2
    me = lax.axis_index("dp")
    lane = lax.axis_index("tensor")
    core = lane % 2
    y = lane // 2
    sibling = y * 2 + (1 - core)
    above = lax.rem(y + 1, n_y) * 2 + core
    below = lax.rem(y + n_y - 1, n_y) * 2 + core

    barrier = pltpu.get_barrier_semaphore()

    def greet(step, carry):
        pl.semaphore_signal(
            barrier,
            inc=1,
            device_id=(lax.rem(me + step, n_dp), lane),
            device_id_type=MESH,
        )
        return carry

    lax.fori_loop(1, n_dp, greet, 0)
    for other in (sibling, above, below):
        pl.semaphore_signal(barrier, inc=1, device_id=(me, other), device_id_type=MESH)

    weight_copies = [
        pltpu.make_async_copy(source, weights.at[:, pl.ds(i * cols, cols)], weight_sem.at[i])
        for i, source in enumerate((w_query, w_key, w_value))
    ]
    for copy in weight_copies:
        copy.start()

    img_r = image_row[...]
    target_r = img_r >> 2
    hit_r = jnp.where(iota((n_dp, tokens), 0) == target_r, 1.0, 0.0)
    upper = jnp.where(
        iota((tokens, tokens), 0) < iota((tokens, tokens), 1), 1.0, 0.0
    ).astype(BF16)
    before_r = dot(hit_r.astype(BF16), upper)
    pos_r = jnp.sum(before_r * hit_r, axis=0, keepdims=True)
    placed_r = target_r.astype(F32) * PAD + pos_r
    img_c = image_col[...]
    target_c = img_c >> 2
    hit_c = jnp.where(iota((tokens, n_dp), 1) == target_c, 1.0, 0.0)
    lower = jnp.where(
        iota((tokens, tokens), 1) < iota((tokens, tokens), 0), 1.0, 0.0
    ).astype(BF16)
    before_c = dot(lower, hit_c.astype(BF16))
    pos_c = jnp.sum(before_c * hit_c, axis=1, keepdims=True)
    position[...] = target_c.astype(F32) * PAD + pos_c

    code_r = ((img_r & 3) + 1).astype(F32)
    shift = (lax.rem(me, TOGETHER) * CAP).astype(F32)
    place = jnp.where(
        iota((tokens, HEAD), 1).astype(F32) == pos_c + shift, 1.0, 0.0
    ).astype(BF16)
    codes[...] = dot((hit_r * code_r).astype(BF16), place)

    tight_out = iota((BLOCK_ROWS, n_blocks * PAD), 0)
    tight_in = iota((BLOCK_ROWS, n_blocks * PAD), 1)
    tight = jnp.where(
        (tight_out == (tight_in >> 4) * CAP + (tight_in & 15)) & ((tight_in & 15) < CAP),
        1.0,
        0.0,
    ).astype(BF16)

    def pack(step, carry):
        some = TOGETHER * PAD
        wanted = (iota((some, tokens), 0) + step * some).astype(F32)
        pick = jnp.where(wanted == placed_r, 1.0, 0.0).astype(BF16)
        parts = [dot(pick, ref[...]).astype(BF16) for ref in (query, key, value, grad)]
        rows = []
        for block in range(n_blocks):
            part = parts[block // heads]
            left = (block % heads) * HEAD
            rows.append(
                jnp.concatenate(
                    [
                        part[i * PAD : (i + 1) * PAD, left : left + HEAD]
                        for i in range(TOGETHER)
                    ],
                    axis=1,
                )
            )
        packed = dot(tight, jnp.concatenate(rows, axis=0))
        code = jnp.concatenate(
            [codes[pl.ds(step * TOGETHER + i, 1), :] for i in range(TOGETHER)], axis=1
        )
        packed = jnp.where(iota(packed.shape, 0) == CODE_ROW, code, packed).astype(BF16)
        for i in range(TOGETHER):
            send[step * TOGETHER + i] = packed[:, i * HEAD : (i + 1) * HEAD]
        return carry

    lax.fori_loop(0, n_groups, pack, 0)

    pl.semaphore_wait(barrier, n_dp + 2)

    def message(place_in, target):
        return pltpu.make_async_remote_copy(
            src_ref=send.at[target],
            dst_ref=recv.at[place_in],
            send_sem=send_sem.at[target],
            recv_sem=recv_sem.at[place_in],
            device_id=(target, lane),
            device_id_type=MESH,
        )

    def start_message(step, carry):
        message(me, lax.rem(me + step, n_dp)).start()
        return carry

    lax.fori_loop(1, n_dp, start_message, 0)
    recv[me] = send[me]
    for copy in weight_copies:
        copy.wait()

    def wait_message(step, carry):
        other = lax.rem(me + step, n_dp)
        message(other, other).wait_recv()
        return carry

    lax.fori_loop(1, n_dp, wait_message, 0)

    for block in range(n_blocks):
        top = block * CAP // 16 * 16
        skip = block * CAP - top
        shape = (GROUP_ROWS, TOGETHER * WINDOW)
        to, source = iota(shape, 0), iota(shape, 1)
        within = (source & (WINDOW - 1)) - skip
        loose = jnp.where(
            (to == (source >> 5) * CAP + within) & (within >= 0) & (within < CAP), 1.0, 0.0
        ).astype(BF16)
        wide = jnp.concatenate(
            [
                jnp.concatenate(
                    [recv[g * TOGETHER + i, top : top + WINDOW, :] for g in range(n_groups)],
                    axis=1,
                )
                for i in range(TOGETHER)
            ],
            axis=0,
        )
        spread = dot(loose, wide).astype(BF16)
        for g in range(n_groups):
            blocks[block, g * GROUP_ROWS : (g + 1) * GROUP_ROWS, :] = spread[
                :, g * HEAD : (g + 1) * HEAD
            ]

    total = None
    for g in range(n_groups):
        tile = recv[g * TOGETHER, CODE_ROW - 12 :, :].astype(F32)
        for i in range(1, TOGETHER):
            tile = tile + recv[g * TOGETHER + i, CODE_ROW - 12 :, :].astype(F32)
        only = jnp.where(iota((16, HEAD), 0) == 12, tile, 0.0).astype(BF16)
        shape = (HEAD, slots)
        there = iota(shape, 0)
        put = jnp.where(
            (iota(shape, 1) == g * GROUP_ROWS + there) & (there < GROUP_ROWS), 1.0, 0.0
        ).astype(BF16)
        term = dot(only, put)
        total = term if total is None else total + term
    code_row = jnp.sum(total, axis=0, keepdims=True)
    mask_row[...] = code_row
    mask_col[...] = jnp.transpose(jnp.broadcast_to(code_row, (HEAD, slots)))

    scale = HEAD ** (-0.5)
    last = ((1,), (1,))

    def attend(head, carry):
        q = blocks[head]
        k = blocks[heads + head]
        v = blocks[2 * heads + head]
        g = blocks[3 * heads + head]
        allowed = mask_col[:, 0:1] == mask_row[...]
        scores = jnp.where(allowed, dot(k, q, last), -1e30)
        highest = jnp.max(scores, axis=0, keepdims=True)
        raised = jnp.exp((scores - highest) * scale)
        attention = raised * (1.0 / jnp.sum(raised, axis=0, keepdims=True))
        grad_prob = dot(v, g, last)
        row_total = jnp.sum(attention * grad_prob, axis=0, keepdims=True)
        dscore = (attention * (grad_prob - row_total) * scale).astype(BF16)
        grad_value = dot(attention.astype(BF16), g).astype(BF16)
        grad_key = dot(dscore, q).astype(BF16)
        grad_query = jnp.transpose(dot(k, dscore, ((0,), (0,)))).astype(BF16)
        half = slots // 2
        for i, result in enumerate((grad_query, grad_key, grad_value)):
            left = pl.multiple_of((i * heads + head) * HEAD, HEAD)
            grads[0, :, pl.ds(left, HEAD)] = result[:half]
            grads[1, :, pl.ds(left, HEAD)] = result[half:]
        return carry

    lax.fori_loop(0, heads, attend, 0)

    def to_sibling(step):
        return pltpu.make_async_remote_copy(
            src_ref=sib_send.at[step],
            dst_ref=sib_recv.at[step],
            send_sem=sib_send_sem.at[step],
            recv_sem=sib_recv_sem.at[step],
            device_id=(me, sibling),
            device_id_type=MESH,
        )

    def project(step):
        for way in range(2):
            if way == 0:
                chunk = lax.rem(y + 2 * n_y - 1 - step, n_y)
            else:
                chunk = lax.rem(y + 1 + step, n_y)
            w = weights[pl.ds(pl.multiple_of(chunk * chip_cols, chip_cols), chip_cols), :]
            half = upward * GROUP_ROWS
            top = way * half
            rows = jnp.concatenate(
                [grads[core, top : top + half, :], grads[1 - core, top : top + half, :]],
                axis=0,
            )
            product = dot(rows, w, last)
            for i in range(upward):
                chain = way * upward + i
                here = product[i * GROUP_ROWS : (i + 1) * GROUP_ROWS]
                there = product[half + i * GROUP_ROWS : half + (i + 1) * GROUP_ROWS]
                own[step, chain] = here
                sib_send[step, chain] = there.astype(BF16)
        to_sibling(step).start()

    def hop(step, chain):
        slot = step * chains + chain
        return pltpu.make_async_remote_copy(
            src_ref=ring_send.at[slot],
            dst_ref=ring_recv.at[slot],
            send_sem=ring_send_sem.at[slot],
            recv_sem=ring_recv_sem.at[slot],
            device_id=(me, above if chain < upward else below),
            device_id_type=MESH,
        )

    def running(step, chain):
        return own[step, chain] + sib_recv[step, chain].astype(F32)

    project(0)
    project(1)
    to_sibling(0).wait_recv()
    for chain in range(chains):
        ring_send[chain] = running(0, chain).astype(BF16)
        hop(0, chain).start()

    def ring_step(step, carry):
        @pl.when(step < n_y - 1)
        def _():
            project(step + 1)

        to_sibling(step).wait_recv()
        for pair in range(upward):
            for chain in (pair, upward + pair):
                hop(step - 1, chain).wait_recv()
                before = (step - 1) * chains + chain
                ring_send[step * chains + chain] = (
                    running(step, chain) + ring_recv[before].astype(F32)
                ).astype(BF16)
                hop(step, chain).start()
        return carry

    lax.fori_loop(1, n_y - 1, ring_step, 0)

    def back(index, target, home):
        return pltpu.make_async_remote_copy(
            src_ref=back_send.at[index],
            dst_ref=back_recv.at[home],
            send_sem=back_send_sem.at[index],
            recv_sem=back_recv_sem.at[home],
            device_id=(target, lane),
            device_id_type=MESH,
        )

    shape = (TOGETHER * PAD, GROUP_ROWS)
    to, source = iota(shape, 0), iota(shape, 1)
    apart = jnp.where(
        (source == (to >> 4) * CAP + (to & 15)) & ((to & 15) < CAP), 1.0, 0.0
    ).astype(BF16)
    to_sibling(n_y - 1).wait_recv()
    for pair in range(upward):
        for chain in (pair, upward + pair):
            hop(n_y - 2, chain).wait_recv()
            before = (n_y - 2) * chains + chain
            final = (running(n_y - 1, chain) + ring_recv[before].astype(F32)).astype(BF16)
            laid = dot(apart, final).astype(BF16)
            for i in range(TOGETHER):
                index = chain * TOGETHER + i
                target = (core * chains + chain) * TOGETHER + i
                back_send[index] = laid[i * PAD : (i + 1) * PAD]

                @pl.when(target != me)
                def _():
                    back(index, target, me).start()

                @pl.when(target == me)
                def _():
                    back_recv[me] = back_send[index]

    half_dp = n_dp // 2
    mine = (me // half_dp) == core

    def to_last():
        return pltpu.make_async_remote_copy(
            src_ref=last_send,
            dst_ref=last_recv,
            send_sem=last_sem.at[0],
            recv_sem=last_sem.at[1],
            device_id=(me, sibling),
            device_id_type=MESH,
        )

    @pl.when(mine)
    def _():
        def wait_back(step, carry):
            home = lax.rem(me + step, n_dp)
            back(0, home, home).wait_recv()
            return carry

        lax.fori_loop(1, n_dp, wait_back, 0)
        width = out.shape[1]
        wide = last_send.shape[1]
        pick = jnp.where(
            iota((tokens, n_dp * PAD), 1).astype(F32) == position[...], 1.0, 0.0
        ).astype(BF16)
        every = back_recv[...].reshape(n_dp * PAD, chip_cols)
        rows = dot(pick, every).astype(BF16)
        shape = (chip_cols, wide)
        from_col, to_col = iota(shape, 0), iota(shape, 1)
        other = jnp.where(
            (from_col == to_col + (1 - core) * width) & (to_col < width), 1.0, 0.0
        ).astype(BF16)
        here = jnp.where(
            (from_col == to_col + core * width) & (to_col < width), 1.0, 0.0
        ).astype(BF16)
        last_send[...] = dot(rows, other).astype(BF16)
        to_last().start()
        out[...] = dot(rows, here)[:, :width].astype(BF16)
        to_last().wait_send()

    @pl.when(jnp.logical_not(mine))
    def _():
        to_last().wait_recv()
        out[...] = last_recv[:, : out.shape[1]]

    def left_message(step, carry):
        other = lax.rem(me + step, n_dp)
        message(other, other).wait_send()
        return carry

    lax.fori_loop(1, n_dp, left_message, 0)

    def left_step(step, carry):
        to_sibling(step).wait_send()
        return carry

    lax.fori_loop(0, n_y, left_step, 0)

    def left_hop(step, carry):
        for chain in range(chains):
            hop(step, chain).wait_send()
        return carry

    lax.fori_loop(0, n_y - 1, left_hop, 0)

    def left_back(index, carry):
        target = core * half_dp + index

        @pl.when(target != me)
        def _():
            back(index, target, me).wait_send()

        return carry

    lax.fori_loop(0, half_dp, left_back, 0)


def shards(query_rows, key_rows, value_rows, out_grad, w_query, w_key, w_value, row_image):
    n_dp = lax.axis_size("dp")
    n_tensor = lax.axis_size("tensor")
    n_y = n_tensor // 2
    tokens, cols = query_rows.shape
    features = w_query.shape[0]
    width = features // n_tensor
    chip_cols = 2 * width
    wide = (width + HEAD - 1) // HEAD * HEAD
    heads = cols // HEAD
    n_groups = n_dp // TOGETHER
    slots = n_groups * GROUP_ROWS
    chains = n_groups // 2
    vmem = pl.BlockSpec(memory_space=pltpu.VMEM)
    hbm = pl.BlockSpec(memory_space=pl.ANY)
    dma = pltpu.SemaphoreType.DMA
    return pl.pallas_call(
        functools.partial(kernel, (n_dp, n_y)),
        out_shape=jax.ShapeDtypeStruct((tokens, width), BF16),
        in_specs=[vmem] * 6 + [hbm] * 3,
        out_specs=vmem,
        scratch_shapes=[
            pltpu.VMEM((n_dp, HEAD), F32),
            pltpu.VMEM((tokens, 1), F32),
            pltpu.VMEM((n_dp, BLOCK_ROWS, HEAD), BF16),
            pltpu.VMEM((n_dp, BLOCK_ROWS, HEAD), BF16),
            pltpu.VMEM((4 * heads, slots, HEAD), BF16),
            pltpu.VMEM((1, slots), F32),
            pltpu.VMEM((slots, HEAD), F32),
            pltpu.VMEM((2, slots // 2, 3 * cols), BF16),
            pltpu.VMEM((features, 3 * cols), BF16),
            pltpu.VMEM((n_y, chains, GROUP_ROWS, chip_cols), F32),
            pltpu.VMEM((n_y, chains, GROUP_ROWS, chip_cols), BF16),
            pltpu.VMEM((n_y, chains, GROUP_ROWS, chip_cols), BF16),
            pltpu.VMEM(((n_y - 1) * chains, GROUP_ROWS, chip_cols), BF16),
            pltpu.VMEM(((n_y - 1) * chains, GROUP_ROWS, chip_cols), BF16),
            pltpu.VMEM((n_dp // 2, PAD, chip_cols), BF16),
            pltpu.VMEM((n_dp, PAD, chip_cols), BF16),
            pltpu.VMEM((tokens, wide), BF16),
            pltpu.VMEM((tokens, wide), BF16),
            dma((n_dp,)),
            dma((n_dp,)),
            dma((3,)),
            dma((n_y,)),
            dma((n_y,)),
            dma(((n_y - 1) * chains,)),
            dma(((n_y - 1) * chains,)),
            dma((n_dp // 2,)),
            dma((n_dp,)),
            dma((2,)),
        ],
        compiler_params=pltpu.CompilerParams(
            collective_id=0, has_side_effects=True, vmem_limit_bytes=56 * 2**20
        ),
    )(
        row_image.reshape(1, tokens),
        row_image.reshape(tokens, 1),
        query_rows,
        key_rows,
        value_rows,
        out_grad,
        w_query,
        w_key,
        w_value,
    )


def solution(mesh):
    placed = (
        P("dp", "tensor"),
        P("dp", "tensor"),
        P("dp", "tensor"),
        P("dp", "tensor"),
        P(None, "tensor"),
        P(None, "tensor"),
        P(None, "tensor"),
        P("dp"),
    )
    return jax.shard_map(
        shards, mesh=mesh, in_specs=placed, out_specs=P("dp", "tensor"), check_vma=False
    )
```

```python
import functools

import jax
import jax.numpy as jnp
from jax import lax
from jax.experimental import pallas as pl
from jax.experimental.pallas import tpu as pltpu
from jax.sharding import PartitionSpec as P

HEAD = 128
IMG_DEV = 4
CAP = 13
PAD = 16
TOGETHER = 6
WINDOW = 32
BLOCK_ROWS = 160
PARTS = ((0, 64), (64, 48), (112, 48))
GROUP_ROWS = 80
MESH = pl.DeviceIdType.MESH
F32 = jnp.float32
BF16 = jnp.bfloat16


def iota(shape, dim):
    return lax.broadcasted_iota(jnp.int32, shape, dim)


def dot(a, b, contract=((1,), (0,))):
    return lax.dot_general(a, b, (contract, ((), ())), preferred_element_type=F32)


def kernel(
    sizes,
    image_row,
    query,
    key,
    value,
    grad,
    w_query,
    w_key,
    w_value,
    out,
    codes,
    position,
    send,
    recv,
    blocks,
    mask_row,
    mask_col,
    grad_mine,
    grad_send,
    grad_recv,
    weights,
    sums,
    ring_send,
    ring_recv,
    back_send,
    back_recv,
    last_send,
    last_recv,
    send_sem,
    recv_sem,
    weight_sem,
    far_send_sem,
    far_recv_sem,
    grad_send_sem,
    grad_recv_sem,
    ring_send_sem,
    ring_recv_sem,
    back_send_sem,
    back_recv_sem,
    last_sem,
):
    n_dp, n_y = sizes
    tokens = query.shape[0]
    cols = query.shape[1]
    heads = cols // HEAD
    n_blocks = 4 * heads
    n_groups = n_dp // TOGETHER
    slots = n_groups * GROUP_ROWS
    half_slots = slots // 2
    chains = n_groups // 2
    upward = chains // 2
    chip_cols = out.shape[1] * 2
    me = lax.axis_index("dp")
    lane = lax.axis_index("tensor")
    core = lane % 2
    y = lane // 2
    sibling = y * 2 + (1 - core)
    above = lax.rem(y + 1, n_y) * 2 + core
    below = lax.rem(y + n_y - 1, n_y) * 2 + core

    barrier = pltpu.get_barrier_semaphore()

    def greet(step, carry):
        pl.semaphore_signal(
            barrier,
            inc=1,
            device_id=(lax.rem(me + step, n_dp), lane),
            device_id_type=MESH,
        )
        return carry

    lax.fori_loop(1, n_dp, greet, 0)
    for other in (sibling, above, below):
        pl.semaphore_signal(barrier, inc=1, device_id=(me, other), device_id_type=MESH)

    sources = (w_query, w_key, w_value)
    weight_copies = [
        pltpu.make_async_copy(
            source, weights.at[0, :, pl.ds(i * cols, cols)], weight_sem.at[i]
        )
        for i, source in enumerate(sources)
    ]
    far_copies = [
        pltpu.make_async_remote_copy(
            src_ref=source,
            dst_ref=weights.at[1, :, pl.ds(i * cols, cols)],
            send_sem=far_send_sem.at[i],
            recv_sem=far_recv_sem.at[i],
            device_id=(me, sibling),
            device_id_type=MESH,
        )
        for i, source in enumerate(sources)
    ]

    img_r = image_row[...]
    target_r = img_r >> 2
    hit_r = jnp.where(iota((n_dp, tokens), 0) == target_r, 1.0, 0.0)
    upper = jnp.where(
        iota((tokens, tokens), 0) < iota((tokens, tokens), 1), 1.0, 0.0
    ).astype(BF16)
    before_r = dot(hit_r.astype(BF16), upper)
    pos_r = jnp.sum(before_r * hit_r, axis=0, keepdims=True)
    placed_r = target_r.astype(F32) * PAD + pos_r
    code_r = ((img_r & 3) + 1).astype(F32)
    shift = (lax.rem(me, TOGETHER) * CAP).astype(F32)
    place = jnp.where(
        iota((HEAD, tokens), 0).astype(F32) == pos_r + shift, 1.0, 0.0
    ).astype(BF16)
    last = ((1,), (1,))
    codes[...] = dot((hit_r * code_r).astype(BF16), place, last)

    tight_out = iota((BLOCK_ROWS, n_blocks * PAD), 0)
    tight_in = iota((BLOCK_ROWS, n_blocks * PAD), 1)
    tight = jnp.where(
        (tight_out == 1 + (tight_in >> 4) * CAP + (tight_in & 15)) & ((tight_in & 15) < CAP),
        1.0,
        0.0,
    ).astype(BF16)

    def message(part, place_in, target):
        rows = pl.ds(*PARTS[part])
        return pltpu.make_async_remote_copy(
            src_ref=send.at[target, rows],
            dst_ref=recv.at[place_in, rows],
            send_sem=send_sem.at[part, target],
            recv_sem=recv_sem.at[part, place_in],
            device_id=(target, lane),
            device_id_type=MESH,
        )

    pl.semaphore_wait(barrier, n_dp + 2)

    def pack(step, carry):
        targets = [lax.rem(me + 1 + step * TOGETHER + i, n_dp) for i in range(TOGETHER)]
        wanted = jnp.concatenate(
            [iota((PAD, tokens), 0) + target * PAD for target in targets], axis=0
        ).astype(F32)
        pick = jnp.where(wanted == placed_r, 1.0, 0.0).astype(BF16)
        parts = [dot(pick, ref[...]).astype(BF16) for ref in (query, key, value, grad)]
        rows = []
        for head in range(heads):
            for part in parts:
                rows.append(
                    jnp.concatenate(
                        [
                            part[i * PAD : (i + 1) * PAD, head * HEAD : (head + 1) * HEAD]
                            for i in range(TOGETHER)
                        ],
                        axis=1,
                    )
                )
        packed = dot(tight, jnp.concatenate(rows, axis=0))
        code = jnp.concatenate([codes[pl.ds(target, 1), :] for target in targets], axis=1)
        packed = jnp.where(iota(packed.shape, 0) == 0, code, packed).astype(BF16)
        for i, target in enumerate(targets):
            send[target] = packed[:, i * HEAD : (i + 1) * HEAD]

            @pl.when(target != me)
            def _():
                message(0, me, target).start()

        return carry

    lax.fori_loop(0, n_groups, pack, 0)
    for copy in weight_copies + far_copies:
        copy.start()
    for part in range(1, heads):

        def start_part(step, carry):
            message(part, me, lax.rem(me + step, n_dp)).start()
            return carry

        lax.fori_loop(1, n_dp, start_part, 0)
    recv[me] = send[me]
    position[...] = jnp.transpose(jnp.broadcast_to(placed_r, (HEAD, tokens)))

    def unpack(head):
        def one(which, carry):
            start = 1 + (head * 4 + which) * CAP
            top = pl.multiple_of(jnp.minimum(start // 16 * 16, BLOCK_ROWS - WINDOW), 16)
            skip = start - top
            shape = (GROUP_ROWS, TOGETHER * WINDOW)
            to, source = iota(shape, 0), iota(shape, 1)
            within = (source & (WINDOW - 1)) - skip
            loose = jnp.where(
                (to == (source >> 5) * CAP + within) & (within >= 0) & (within < CAP),
                1.0,
                0.0,
            ).astype(BF16)
            wide = jnp.concatenate(
                [
                    jnp.concatenate(
                        [
                            recv[g * TOGETHER + i, pl.ds(top, WINDOW), :]
                            for g in range(n_groups)
                        ],
                        axis=1,
                    )
                    for i in range(TOGETHER)
                ],
                axis=0,
            )
            spread = dot(loose, wide).astype(BF16)
            for g in range(n_groups):
                blocks[which, g * GROUP_ROWS : (g + 1) * GROUP_ROWS, :] = spread[
                    :, g * HEAD : (g + 1) * HEAD
                ]
            return carry

        lax.fori_loop(0, 4, one, 0)

    def codes_in():
        total = None
        for g in range(n_groups):
            tile = recv[g * TOGETHER, :16, :].astype(F32)
            for i in range(1, TOGETHER):
                tile = tile + recv[g * TOGETHER + i, :16, :].astype(F32)
            only = jnp.where(iota((16, HEAD), 0) == 0, tile, 0.0).astype(BF16)
            shape = (HEAD, slots)
            there = iota(shape, 0)
            put = jnp.where(
                (iota(shape, 1) == g * GROUP_ROWS + there) & (there < GROUP_ROWS), 1.0, 0.0
            ).astype(BF16)
            term = dot(only, put)
            total = term if total is None else total + term
        code_row = jnp.sum(total, axis=0, keepdims=True)
        mask_row[...] = code_row
        mask_col[...] = jnp.transpose(jnp.broadcast_to(code_row, (HEAD, slots)))

    scale = HEAD ** (-0.5)

    def to_sibling(head):
        return pltpu.make_async_remote_copy(
            src_ref=grad_send.at[head],
            dst_ref=grad_recv.at[head],
            send_sem=grad_send_sem.at[head],
            recv_sem=grad_recv_sem.at[head],
            device_id=(me, sibling),
            device_id_type=MESH,
        )

    def attend(head):
        q = blocks[0]
        k = blocks[1]
        v = blocks[2]
        g = blocks[3]
        allowed = mask_col[:, 0:1] == mask_row[...]
        scores = jnp.where(allowed, dot(k, q, last), -1e30)
        highest = jnp.max(scores, axis=0, keepdims=True)
        raised = jnp.exp((scores - highest) * scale)
        attention = raised * (1.0 / jnp.sum(raised, axis=0, keepdims=True))
        grad_prob = dot(v, g, last)
        row_total = jnp.sum(attention * grad_prob, axis=0, keepdims=True)
        dscore = (attention * (grad_prob - row_total) * scale).astype(BF16)
        grad_value = dot(attention.astype(BF16), g).astype(BF16)
        grad_key = dot(dscore, q).astype(BF16)
        grad_query = jnp.transpose(dot(k, dscore, ((0,), (0,)))).astype(BF16)
        first = core == 0
        for i, result in enumerate((grad_query, grad_key, grad_value)):
            low, high = result[:half_slots], result[half_slots:]
            left = slice(i * HEAD, (i + 1) * HEAD)
            grad_mine[head, :, left] = jnp.where(first, low, high)
            grad_send[head, :, left] = jnp.where(first, high, low)
        to_sibling(head).start()

    def chunk_of(o):
        ahead = (n_y - o) // 2
        return lax.rem(y + n_y + jnp.where(o % 2 == 1, -ahead, ahead), n_y)

    def product(source, owner, o, some):
        left = pl.multiple_of(chunk_of(o) * chip_cols, chip_cols)
        rows = jnp.concatenate([source[head] for head in some], axis=1)
        w = jnp.concatenate(
            [
                weights[
                    owner,
                    pl.ds(left, chip_cols),
                    i * cols + head * HEAD : i * cols + (head + 1) * HEAD,
                ]
                for head in some
                for i in range(3)
            ],
            axis=1,
        )
        return dot(rows, w, last)

    def project_first(o, carry):
        early = range(heads - 1)
        sums[o] = product(grad_mine, 0, o, early) + product(grad_recv, 1, o, early)
        return carry

    def project_last(o, carry):
        some = (heads - 1,)
        sums[o] += product(grad_mine, 0, o, some) + product(grad_recv, 1, o, some)
        return carry

    def one_head(head, carry):
        for part in range(heads):

            @pl.when(head == part)
            def _():
                def wait_part(step, carry):
                    other = lax.rem(me + step, n_dp)
                    message(part, other, other).wait_recv()
                    return carry

                lax.fori_loop(1, n_dp, wait_part, 0)

        unpack(head)
        pl.when(head == 0)(codes_in)
        attend(head)

        @pl.when(head == heads - 2)
        def _():
            for copy in weight_copies:
                copy.wait()
            for copy in far_copies:
                copy.wait_recv()
            for early in range(heads - 1):
                to_sibling(early).wait_recv()
            lax.fori_loop(0, n_y, project_first, 0)

        return carry

    lax.fori_loop(0, heads, one_head, 0)

    reach = n_y // 2
    first_set = range(upward)
    second_set = range(upward, chains)

    def hop(way, step, chain):
        slot = (way * reach + step) * chains + chain
        return pltpu.make_async_remote_copy(
            src_ref=ring_send.at[slot],
            dst_ref=ring_recv.at[slot],
            send_sem=ring_send_sem.at[slot],
            recv_sem=ring_recv_sem.at[slot],
            device_id=(me, above if way else below),
            device_id_type=MESH,
        )

    def rows_of(o, chain):
        return sums[o, chain * GROUP_ROWS : (chain + 1) * GROUP_ROWS, :]

    def arrived(way, step, chain):
        hop(way, step, chain).wait_recv()
        return ring_recv[(way * reach + step) * chains + chain].astype(F32)

    def first_hop(way, chain, o):
        ring_send[way * reach * chains + chain] = rows_of(o, chain).astype(BF16)
        hop(way, 0, chain).start()

    def next_hop(way, step, chain, o):
        slot = (way * reach + step) * chains + chain
        ring_send[slot] = (rows_of(o, chain) + arrived(way, step - 1, chain)).astype(BF16)
        hop(way, step, chain).start()

    to_sibling(heads - 1).wait_recv()
    project_last(0, 0)
    for down, up in zip(first_set, second_set):
        first_hop(0, down, 0)
        first_hop(1, up, 0)
    lax.fori_loop(1, 3, project_last, 0)
    for down, up in zip(second_set, first_set):
        first_hop(0, down, 1)
        first_hop(1, up, 2)

    def ring_step(step, carry):
        for down, up in zip(first_set, second_set):
            next_hop(0, step, down, 2 * step - 1)
            next_hop(1, step, up, 2 * step)
        lax.fori_loop(2 * step + 1, jnp.minimum(2 * step + 3, n_y), project_last, 0)

        @pl.when(step < reach - 1)
        def _():
            for down, up in zip(second_set, first_set):
                next_hop(0, step, down, 2 * step + 1)
                next_hop(1, step, up, 2 * step + 2)

        return carry

    lax.fori_loop(1, reach, ring_step, 0)

    def back(index, target, home):
        return pltpu.make_async_remote_copy(
            src_ref=back_send.at[index],
            dst_ref=back_recv.at[home],
            send_sem=back_send_sem.at[index],
            recv_sem=back_recv_sem.at[home],
            device_id=(target, lane),
            device_id_type=MESH,
        )

    shape = (TOGETHER * PAD, GROUP_ROWS)
    to, source = iota(shape, 0), iota(shape, 1)
    apart = jnp.where(
        (source == (to >> 4) * CAP + (to & 15)) & ((to & 15) < CAP), 1.0, 0.0
    ).astype(BF16)
    for pair in range(upward):
        for chain in (pair, upward + pair):
            longer = 0 if chain in first_set else 1
            final = rows_of(n_y - 1, chain) + arrived(1 - longer, reach - 2, chain)
            final = (final + arrived(longer, reach - 1, chain)).astype(BF16)
            laid = dot(apart, final).astype(BF16)
            for i in range(TOGETHER):
                index = chain * TOGETHER + i
                target = (core * chains + chain) * TOGETHER + i
                back_send[index] = laid[i * PAD : (i + 1) * PAD]

                @pl.when(target != me)
                def _():
                    back(index, target, me).start()

                @pl.when(target == me)
                def _():
                    back_recv[me] = back_send[index]

    half_dp = n_dp // 2
    mine = (me // half_dp) == core

    def to_last():
        return pltpu.make_async_remote_copy(
            src_ref=last_send,
            dst_ref=last_recv,
            send_sem=last_sem.at[0],
            recv_sem=last_sem.at[1],
            device_id=(me, sibling),
            device_id_type=MESH,
        )

    for part in range(heads):

        def left_part(step, carry):
            other = lax.rem(me + step, n_dp)
            message(part, other, other).wait_send()
            return carry

        lax.fori_loop(1, n_dp, left_part, 0)
    for copy in far_copies:
        copy.wait_send()
    for head in range(heads):
        to_sibling(head).wait_send()

    def left_hop(step, carry):
        for chain in range(chains):
            hop(0, step, chain).wait_send()
            hop(1, step, chain).wait_send()
        return carry

    lax.fori_loop(0, reach - 1, left_hop, 0)
    for down, up in zip(first_set, second_set):
        hop(0, reach - 1, down).wait_send()
        hop(1, reach - 1, up).wait_send()

    def left_back(index, carry):
        target = core * half_dp + index

        @pl.when(target != me)
        def _():
            back(index, target, me).wait_send()

        return carry

    lax.fori_loop(0, half_dp, left_back, 0)

    @pl.when(mine)
    def _():
        width = out.shape[1]
        wide = last_send.shape[1]
        pick = jnp.where(
            iota((tokens, n_dp * PAD), 1).astype(F32) == position[:, 0:1], 1.0, 0.0
        ).astype(BF16)
        shape = (chip_cols, wide)
        from_col, to_col = iota(shape, 0), iota(shape, 1)
        other = jnp.where(
            (from_col == to_col + (1 - core) * width) & (to_col < width), 1.0, 0.0
        ).astype(BF16)
        here = jnp.where(
            (from_col == to_col + core * width) & (to_col < width), 1.0, 0.0
        ).astype(BF16)

        def wait_back(step, carry):
            home = lax.rem(me + step, n_dp)
            back(0, home, home).wait_recv()
            return carry

        lax.fori_loop(1, n_dp, wait_back, 0)
        every = back_recv[...].reshape(n_dp * PAD, chip_cols)
        rows = dot(pick, every).astype(BF16)
        last_send[...] = dot(rows, other).astype(BF16)
        to_last().start()
        out[...] = dot(rows, here)[:, :width].astype(BF16)
        to_last().wait_send()

    @pl.when(jnp.logical_not(mine))
    def _():
        to_last().wait_recv()
        out[...] = last_recv[:, : out.shape[1]]


def shards(query_rows, key_rows, value_rows, out_grad, w_query, w_key, w_value, row_image):
    n_dp = lax.axis_size("dp")
    n_tensor = lax.axis_size("tensor")
    n_y = n_tensor // 2
    tokens, cols = query_rows.shape
    features = w_query.shape[0]
    width = features // n_tensor
    chip_cols = 2 * width
    wide = (width + HEAD - 1) // HEAD * HEAD
    heads = cols // HEAD
    n_groups = n_dp // TOGETHER
    slots = n_groups * GROUP_ROWS
    chains = n_groups // 2
    hops = n_y * chains
    vmem = pl.BlockSpec(memory_space=pltpu.VMEM)
    hbm = pl.BlockSpec(memory_space=pl.ANY)
    dma = pltpu.SemaphoreType.DMA
    return pl.pallas_call(
        functools.partial(kernel, (n_dp, n_y)),
        out_shape=jax.ShapeDtypeStruct((tokens, width), BF16),
        in_specs=[vmem] * 5 + [hbm] * 3,
        out_specs=vmem,
        scratch_shapes=[
            pltpu.VMEM((n_dp, HEAD), F32),
            pltpu.VMEM((tokens, HEAD), F32),
            pltpu.VMEM((n_dp, BLOCK_ROWS, HEAD), BF16),
            pltpu.VMEM((n_dp, BLOCK_ROWS, HEAD), BF16),
            pltpu.VMEM((4, slots, HEAD), BF16),
            pltpu.VMEM((1, slots), F32),
            pltpu.VMEM((slots, HEAD), F32),
            pltpu.VMEM((heads, slots // 2, 3 * HEAD), BF16),
            pltpu.VMEM((heads, slots // 2, 3 * HEAD), BF16),
            pltpu.VMEM((heads, slots // 2, 3 * HEAD), BF16),
            pltpu.VMEM((2, features, 3 * cols), BF16),
            pltpu.VMEM((n_y, slots // 2, chip_cols), F32),
            pltpu.VMEM((hops, GROUP_ROWS, chip_cols), BF16),
            pltpu.VMEM((hops, GROUP_ROWS, chip_cols), BF16),
            pltpu.VMEM((n_dp // 2, PAD, chip_cols), BF16),
            pltpu.VMEM((n_dp, PAD, chip_cols), BF16),
            pltpu.VMEM((tokens, wide), BF16),
            pltpu.VMEM((tokens, wide), BF16),
            dma((heads, n_dp)),
            dma((heads, n_dp)),
            dma((3,)),
            dma((3,)),
            dma((3,)),
            dma((heads,)),
            dma((heads,)),
            dma((hops,)),
            dma((hops,)),
            dma((n_dp // 2,)),
            dma((n_dp,)),
            dma((2,)),
        ],
        compiler_params=pltpu.CompilerParams(
            collective_id=0, has_side_effects=True, vmem_limit_bytes=56 * 2**20
        ),
    )(
        row_image.reshape(1, tokens),
        query_rows,
        key_rows,
        value_rows,
        out_grad,
        w_query,
        w_key,
        w_value,
    )


def solution(mesh):
    placed = (
        P("dp", "tensor"),
        P("dp", "tensor"),
        P("dp", "tensor"),
        P("dp", "tensor"),
        P(None, "tensor"),
        P(None, "tensor"),
        P(None, "tensor"),
        P("dp"),
    )
    return jax.shard_map(
        shards, mesh=mesh, in_specs=placed, out_specs=P("dp", "tensor"), check_vma=False
    )
```

```python
import functools

import jax
import jax.numpy as jnp
from jax import lax
from jax.experimental import pallas as pl
from jax.experimental.pallas import tpu as pltpu
from jax.sharding import PartitionSpec as P

HEAD = 128
IMG_DEV = 4
CAP = 13
PAD = 16
TOGETHER = 6
WINDOW = 32
BLOCK_ROWS = 160
PARTS = ((0, 112), (112, 48))
GROUP_ROWS = 80
MESH = pl.DeviceIdType.MESH
F32 = jnp.float32
BF16 = jnp.bfloat16


def iota(shape, dim):
    return lax.broadcasted_iota(jnp.int32, shape, dim)


def dot(a, b, contract=((1,), (0,))):
    return lax.dot_general(a, b, (contract, ((), ())), preferred_element_type=F32)


def kernel(
    sizes,
    image_row,
    query,
    key,
    value,
    grad,
    w_query,
    w_key,
    w_value,
    out,
    rows_in,
    codes,
    position,
    send,
    recv,
    blocks,
    mask_row,
    mask_col,
    grad_mine,
    grad_send,
    grad_recv,
    weights,
    sums,
    ring_send,
    ring_recv,
    back_send,
    back_recv,
    last_send,
    last_recv,
    row_sem,
    send_sem,
    recv_sem,
    weight_sem,
    far_send_sem,
    far_recv_sem,
    grad_send_sem,
    grad_recv_sem,
    ring_send_sem,
    ring_recv_sem,
    back_send_sem,
    back_recv_sem,
    last_sem,
):
    n_dp, n_y = sizes
    tokens = query.shape[0]
    cols = query.shape[1]
    heads = cols // HEAD
    n_blocks = 4 * heads
    n_groups = n_dp // TOGETHER
    slots = n_groups * GROUP_ROWS
    half_slots = slots // 2
    chains = n_groups // 2
    upward = chains // 2
    chip_cols = out.shape[1] * 2
    me = lax.axis_index("dp")
    lane = lax.axis_index("tensor")
    core = lane % 2
    y = lane // 2
    sibling = y * 2 + (1 - core)
    above = lax.rem(y + 1, n_y) * 2 + core
    below = lax.rem(y + n_y - 1, n_y) * 2 + core

    barrier = pltpu.get_barrier_semaphore()

    def greet(step, carry):
        pl.semaphore_signal(
            barrier,
            inc=1,
            device_id=(lax.rem(me + step, n_dp), lane),
            device_id_type=MESH,
        )
        return carry

    lax.fori_loop(1, n_dp, greet, 0)
    for other in (sibling, above, below):
        pl.semaphore_signal(barrier, inc=1, device_id=(me, other), device_id_type=MESH)

    row_copies = [
        pltpu.make_async_copy(source, rows_in.at[i], row_sem.at[i])
        for i, source in enumerate((query, key, value, grad))
    ]
    for copy in row_copies:
        copy.start()

    sources = (w_query, w_key, w_value)
    weight_copies = [
        pltpu.make_async_copy(
            source, weights.at[0, :, pl.ds(i * cols, cols)], weight_sem.at[i]
        )
        for i, source in enumerate(sources)
    ]
    far_copies = [
        pltpu.make_async_remote_copy(
            src_ref=source,
            dst_ref=weights.at[1, :, pl.ds(i * cols, cols)],
            send_sem=far_send_sem.at[i],
            recv_sem=far_recv_sem.at[i],
            device_id=(me, sibling),
            device_id_type=MESH,
        )
        for i, source in enumerate(sources)
    ]

    img_r = image_row[...]
    target_r = img_r >> 2
    hit_r = jnp.where(iota((n_dp, tokens), 0) == target_r, 1.0, 0.0)
    upper = jnp.where(
        iota((tokens, tokens), 0) < iota((tokens, tokens), 1), 1.0, 0.0
    ).astype(BF16)
    before_r = dot(hit_r.astype(BF16), upper)
    pos_r = jnp.sum(before_r * hit_r, axis=0, keepdims=True)
    placed_r = target_r.astype(F32) * PAD + pos_r
    code_r = ((img_r & 3) + 1).astype(F32)
    shift = (lax.rem(me, TOGETHER) * CAP).astype(F32)
    place = jnp.where(
        iota((HEAD, tokens), 0).astype(F32) == pos_r + shift, 1.0, 0.0
    ).astype(BF16)
    last = ((1,), (1,))
    codes[...] = dot((hit_r * code_r).astype(BF16), place, last)

    tight_out = iota((BLOCK_ROWS, n_blocks * PAD), 0)
    tight_in = iota((BLOCK_ROWS, n_blocks * PAD), 1)
    tight = jnp.where(
        (tight_out == 1 + (tight_in >> 4) * CAP + (tight_in & 15)) & ((tight_in & 15) < CAP),
        1.0,
        0.0,
    ).astype(BF16)

    def message(part, place_in, target):
        rows = pl.ds(*PARTS[part])
        return pltpu.make_async_remote_copy(
            src_ref=send.at[target, rows],
            dst_ref=recv.at[place_in, rows],
            send_sem=send_sem.at[part, target],
            recv_sem=recv_sem.at[part, place_in],
            device_id=(target, lane),
            device_id_type=MESH,
        )

    def target_of(k):
        away = k // 2 + 1
        away = jnp.where(k % 2 == 0, away, n_dp - away)
        return lax.rem(me + jnp.where(k == n_dp - 1, 0, away), n_dp)

    for copy in row_copies:
        copy.wait()
    pl.semaphore_wait(barrier, n_dp + 2)

    def pack(step, carry):
        targets = [target_of(step * TOGETHER + i) for i in range(TOGETHER)]
        wanted = jnp.concatenate(
            [iota((PAD, tokens), 0) + target * PAD for target in targets], axis=0
        ).astype(F32)
        pick = jnp.where(wanted == placed_r, 1.0, 0.0).astype(BF16)
        parts = [dot(pick, ref[...]).astype(BF16) for ref in (rows_in.at[n] for n in range(4))]
        rows = []
        for head in range(heads):
            for part in parts:
                rows.append(
                    jnp.concatenate(
                        [
                            part[i * PAD : (i + 1) * PAD, head * HEAD : (head + 1) * HEAD]
                            for i in range(TOGETHER)
                        ],
                        axis=1,
                    )
                )
        packed = dot(tight, jnp.concatenate(rows, axis=0))
        code = jnp.concatenate([codes[pl.ds(target, 1), :] for target in targets], axis=1)
        packed = jnp.where(iota(packed.shape, 0) == 0, code, packed).astype(BF16)
        for i, target in enumerate(targets):
            send[target] = packed[:, i * HEAD : (i + 1) * HEAD]

            @pl.when(target != me)
            def _():
                message(0, me, target).start()

        return carry

    lax.fori_loop(0, n_groups, pack, 0)
    for copy in weight_copies + far_copies:
        copy.start()
    for part in range(1, len(PARTS)):

        def start_part(step, carry):
            message(part, me, target_of(step)).start()
            return carry

        lax.fori_loop(0, n_dp - 1, start_part, 0)
    recv[me] = send[me]
    position[...] = jnp.transpose(jnp.broadcast_to(placed_r, (HEAD, tokens)))

    def unpack(head):
        def one(which, carry):
            start = 1 + (head * 4 + which) * CAP
            top = pl.multiple_of(jnp.minimum(start // 16 * 16, BLOCK_ROWS - WINDOW), 16)
            skip = start - top
            shape = (GROUP_ROWS, TOGETHER * WINDOW)
            to, source = iota(shape, 0), iota(shape, 1)
            within = (source & (WINDOW - 1)) - skip
            loose = jnp.where(
                (to == (source >> 5) * CAP + within) & (within >= 0) & (within < CAP),
                1.0,
                0.0,
            ).astype(BF16)
            wide = jnp.concatenate(
                [
                    jnp.concatenate(
                        [
                            recv[g * TOGETHER + i, pl.ds(top, WINDOW), :]
                            for g in range(n_groups)
                        ],
                        axis=1,
                    )
                    for i in range(TOGETHER)
                ],
                axis=0,
            )
            spread = dot(loose, wide).astype(BF16)
            for g in range(n_groups):
                blocks[which, g * GROUP_ROWS : (g + 1) * GROUP_ROWS, :] = spread[
                    :, g * HEAD : (g + 1) * HEAD
                ]
            return carry

        lax.fori_loop(0, 4, one, 0)

    def codes_in():
        total = None
        for g in range(n_groups):
            tile = recv[g * TOGETHER, :16, :].astype(F32)
            for i in range(1, TOGETHER):
                tile = tile + recv[g * TOGETHER + i, :16, :].astype(F32)
            only = jnp.where(iota((16, HEAD), 0) == 0, tile, 0.0).astype(BF16)
            shape = (HEAD, slots)
            there = iota(shape, 0)
            put = jnp.where(
                (iota(shape, 1) == g * GROUP_ROWS + there) & (there < GROUP_ROWS), 1.0, 0.0
            ).astype(BF16)
            term = dot(only, put)
            total = term if total is None else total + term
        code_row = jnp.sum(total, axis=0, keepdims=True)
        mask_row[...] = code_row
        mask_col[...] = jnp.transpose(jnp.broadcast_to(code_row, (HEAD, slots)))

    scale = HEAD ** (-0.5)

    def to_sibling(head):
        return pltpu.make_async_remote_copy(
            src_ref=grad_send.at[head],
            dst_ref=grad_recv.at[head],
            send_sem=grad_send_sem.at[head],
            recv_sem=grad_recv_sem.at[head],
            device_id=(me, sibling),
            device_id_type=MESH,
        )

    def attend(head):
        q = blocks[0]
        k = blocks[1]
        v = blocks[2]
        g = blocks[3]
        allowed = mask_col[:, 0:1] == mask_row[...]
        scores = jnp.where(allowed, dot(k, q, last), -1e30)
        highest = jnp.max(scores, axis=0, keepdims=True)
        raised = jnp.exp((scores - highest) * scale)
        attention = raised * (1.0 / jnp.sum(raised, axis=0, keepdims=True))
        grad_prob = dot(v, g, last)
        row_total = jnp.sum(attention * grad_prob, axis=0, keepdims=True)
        dscore = (attention * (grad_prob - row_total) * scale).astype(BF16)
        grad_value = dot(attention.astype(BF16), g).astype(BF16)
        grad_key = dot(dscore, q).astype(BF16)
        grad_query = jnp.transpose(dot(k, dscore, ((0,), (0,)))).astype(BF16)
        first = core == 0
        for i, result in enumerate((grad_query, grad_key, grad_value)):
            low, high = result[:half_slots], result[half_slots:]
            left = slice(i * HEAD, (i + 1) * HEAD)
            grad_mine[head, :, left] = jnp.where(first, low, high)
            grad_send[head, :, left] = jnp.where(first, high, low)
        to_sibling(head).start()

    def chunk_of(o):
        ahead = (n_y - o) // 2
        return lax.rem(y + n_y + jnp.where(o % 2 == 1, -ahead, ahead), n_y)

    def product(source, owner, o, some):
        left = pl.multiple_of(chunk_of(o) * chip_cols, chip_cols)
        rows = jnp.concatenate([source[head] for head in some], axis=1)
        w = jnp.concatenate(
            [
                weights[
                    owner,
                    pl.ds(left, chip_cols),
                    i * cols + head * HEAD : i * cols + (head + 1) * HEAD,
                ]
                for head in some
                for i in range(3)
            ],
            axis=1,
        )
        return dot(rows, w, last)

    def project_first(o, carry):
        early = range(heads - 1)
        sums[o] = product(grad_mine, 0, o, early) + product(grad_recv, 1, o, early)
        return carry

    def project_last(o, carry):
        some = (heads - 1,)
        sums[o] += product(grad_mine, 0, o, some) + product(grad_recv, 1, o, some)
        return carry

    def one_head(head, carry):
        for part in range(len(PARTS)):

            @pl.when(head == part * (heads - 1))
            def _():
                def wait_part(step, carry):
                    other = lax.rem(me + step, n_dp)
                    message(part, other, other).wait_recv()
                    return carry

                lax.fori_loop(1, n_dp, wait_part, 0)

        unpack(head)
        pl.when(head == 0)(codes_in)
        attend(head)

        @pl.when(head == heads - 2)
        def _():
            for copy in weight_copies:
                copy.wait()
            for copy in far_copies:
                copy.wait_recv()
            for early in range(heads - 1):
                to_sibling(early).wait_recv()
            lax.fori_loop(0, n_y, project_first, 0)

        return carry

    lax.fori_loop(0, heads, one_head, 0)

    reach = n_y // 2
    first_set = range(upward)
    second_set = range(upward, chains)

    def hop(way, step, chain):
        slot = (way * reach + step) * chains + chain
        return pltpu.make_async_remote_copy(
            src_ref=ring_send.at[slot],
            dst_ref=ring_recv.at[slot],
            send_sem=ring_send_sem.at[slot],
            recv_sem=ring_recv_sem.at[slot],
            device_id=(me, above if way else below),
            device_id_type=MESH,
        )

    def rows_of(o, chain):
        return sums[o, chain * GROUP_ROWS : (chain + 1) * GROUP_ROWS, :]

    def arrived(way, step, chain):
        hop(way, step, chain).wait_recv()
        return ring_recv[(way * reach + step) * chains + chain].astype(F32)

    def first_hop(way, chain, o):
        ring_send[way * reach * chains + chain] = rows_of(o, chain).astype(BF16)
        hop(way, 0, chain).start()

    def next_hop(way, step, chain, o):
        slot = (way * reach + step) * chains + chain
        ring_send[slot] = (rows_of(o, chain) + arrived(way, step - 1, chain)).astype(BF16)
        hop(way, step, chain).start()

    to_sibling(heads - 1).wait_recv()
    project_last(0, 0)
    for down, up in zip(first_set, second_set):
        first_hop(0, down, 0)
        first_hop(1, up, 0)
    lax.fori_loop(1, 3, project_last, 0)
    for down, up in zip(second_set, first_set):
        first_hop(0, down, 1)
        first_hop(1, up, 2)

    def ring_step(step, carry):
        for down, up in zip(first_set, second_set):
            next_hop(0, step, down, 2 * step - 1)
            next_hop(1, step, up, 2 * step)
        lax.fori_loop(2 * step + 1, jnp.minimum(2 * step + 3, n_y), project_last, 0)

        @pl.when(step < reach - 1)
        def _():
            for down, up in zip(second_set, first_set):
                next_hop(0, step, down, 2 * step + 1)
                next_hop(1, step, up, 2 * step + 2)

        return carry

    lax.fori_loop(1, reach, ring_step, 0)

    def back(index, target, home):
        return pltpu.make_async_remote_copy(
            src_ref=back_send.at[index],
            dst_ref=back_recv.at[home],
            send_sem=back_send_sem.at[index],
            recv_sem=back_recv_sem.at[home],
            device_id=(target, lane),
            device_id_type=MESH,
        )

    shape = (TOGETHER * PAD, GROUP_ROWS)
    to, source = iota(shape, 0), iota(shape, 1)
    apart = jnp.where(
        (source == (to >> 4) * CAP + (to & 15)) & ((to & 15) < CAP), 1.0, 0.0
    ).astype(BF16)
    for pair in range(upward):
        for chain in (pair, upward + pair):
            longer = 0 if chain in first_set else 1
            final = rows_of(n_y - 1, chain) + arrived(1 - longer, reach - 2, chain)
            final = (final + arrived(longer, reach - 1, chain)).astype(BF16)
            laid = dot(apart, final).astype(BF16)
            for i in range(TOGETHER):
                index = chain * TOGETHER + i
                target = (core * chains + chain) * TOGETHER + i
                back_send[index] = laid[i * PAD : (i + 1) * PAD]

                @pl.when(target != me)
                def _():
                    back(index, target, me).start()

                @pl.when(target == me)
                def _():
                    back_recv[me] = back_send[index]

    half_dp = n_dp // 2
    mine = (me // half_dp) == core

    def to_last():
        return pltpu.make_async_remote_copy(
            src_ref=last_send,
            dst_ref=last_recv,
            send_sem=last_sem.at[0],
            recv_sem=last_sem.at[1],
            device_id=(me, sibling),
            device_id_type=MESH,
        )

    for part in range(len(PARTS)):

        def left_part(step, carry):
            other = lax.rem(me + step, n_dp)
            message(part, other, other).wait_send()
            return carry

        lax.fori_loop(1, n_dp, left_part, 0)
    for copy in far_copies:
        copy.wait_send()
    for head in range(heads):
        to_sibling(head).wait_send()

    def left_hop(step, carry):
        for chain in range(chains):
            hop(0, step, chain).wait_send()
            hop(1, step, chain).wait_send()
        return carry

    lax.fori_loop(0, reach - 1, left_hop, 0)
    for down, up in zip(first_set, second_set):
        hop(0, reach - 1, down).wait_send()
        hop(1, reach - 1, up).wait_send()

    def left_back(index, carry):
        target = core * half_dp + index

        @pl.when(target != me)
        def _():
            back(index, target, me).wait_send()

        return carry

    lax.fori_loop(0, half_dp, left_back, 0)

    @pl.when(mine)
    def _():
        width = out.shape[1]
        wide = last_send.shape[1]
        pick = jnp.where(
            iota((tokens, n_dp * PAD), 1).astype(F32) == position[:, 0:1], 1.0, 0.0
        ).astype(BF16)
        def wait_back(step, carry):
            home = lax.rem(me + step, n_dp)
            back(0, home, home).wait_recv()
            return carry

        lax.fori_loop(1, n_dp, wait_back, 0)
        every = back_recv[...].reshape(n_dp * PAD, chip_cols)
        rows = dot(pick, every)

        @pl.when(core == 0)
        def _():
            last_send[...] = rows[:, chip_cols - wide :].astype(BF16)
            to_last().start()
            out[...] = rows[:, :width].astype(BF16)

        @pl.when(core == 1)
        def _():
            last_send[...] = rows[:, :wide].astype(BF16)
            to_last().start()
            out[...] = rows[:, width:].astype(BF16)

        to_last().wait_send()

    @pl.when(jnp.logical_not(mine))
    def _():
        width = out.shape[1]
        wide = last_recv.shape[1]
        to_last().wait_recv()

        @pl.when(core == 0)
        def _():
            out[...] = last_recv[:, :width]

        @pl.when(core == 1)
        def _():
            out[...] = last_recv[:, wide - width :]


def shards(query_rows, key_rows, value_rows, out_grad, w_query, w_key, w_value, row_image):
    n_dp = lax.axis_size("dp")
    n_tensor = lax.axis_size("tensor")
    n_y = n_tensor // 2
    tokens, cols = query_rows.shape
    features = w_query.shape[0]
    width = features // n_tensor
    chip_cols = 2 * width
    wide = (width + HEAD - 1) // HEAD * HEAD
    heads = cols // HEAD
    n_groups = n_dp // TOGETHER
    slots = n_groups * GROUP_ROWS
    chains = n_groups // 2
    hops = n_y * chains
    vmem = pl.BlockSpec(memory_space=pltpu.VMEM)
    hbm = pl.BlockSpec(memory_space=pl.ANY)
    dma = pltpu.SemaphoreType.DMA
    return pl.pallas_call(
        functools.partial(kernel, (n_dp, n_y)),
        out_shape=jax.ShapeDtypeStruct((tokens, width), BF16),
        in_specs=[vmem] + [hbm] * 7,
        out_specs=vmem,
        scratch_shapes=[
            pltpu.VMEM((4, tokens, cols), BF16),
            pltpu.VMEM((n_dp, HEAD), F32),
            pltpu.VMEM((tokens, HEAD), F32),
            pltpu.VMEM((n_dp, BLOCK_ROWS, HEAD), BF16),
            pltpu.VMEM((n_dp, BLOCK_ROWS, HEAD), BF16),
            pltpu.VMEM((4, slots, HEAD), BF16),
            pltpu.VMEM((1, slots), F32),
            pltpu.VMEM((slots, HEAD), F32),
            pltpu.VMEM((heads, slots // 2, 3 * HEAD), BF16),
            pltpu.VMEM((heads, slots // 2, 3 * HEAD), BF16),
            pltpu.VMEM((heads, slots // 2, 3 * HEAD), BF16),
            pltpu.VMEM((2, features, 3 * cols), BF16),
            pltpu.VMEM((n_y, slots // 2, chip_cols), F32),
            pltpu.VMEM((hops, GROUP_ROWS, chip_cols), BF16),
            pltpu.VMEM((hops, GROUP_ROWS, chip_cols), BF16),
            pltpu.VMEM((n_dp // 2, PAD, chip_cols), BF16),
            pltpu.VMEM((n_dp, PAD, chip_cols), BF16),
            pltpu.VMEM((tokens, wide), BF16),
            pltpu.VMEM((tokens, wide), BF16),
            dma((4,)),
            dma((len(PARTS), n_dp)),
            dma((len(PARTS), n_dp)),
            dma((3,)),
            dma((3,)),
            dma((3,)),
            dma((heads,)),
            dma((heads,)),
            dma((hops,)),
            dma((hops,)),
            dma((n_dp // 2,)),
            dma((n_dp,)),
            dma((2,)),
        ],
        compiler_params=pltpu.CompilerParams(
            collective_id=0, has_side_effects=True, vmem_limit_bytes=56 * 2**20
        ),
    )(
        row_image.reshape(1, tokens),
        query_rows,
        key_rows,
        value_rows,
        out_grad,
        w_query,
        w_key,
        w_value,
    )


def solution(mesh):
    placed = (
        P("dp", "tensor"),
        P("dp", "tensor"),
        P("dp", "tensor"),
        P("dp", "tensor"),
        P(None, "tensor"),
        P(None, "tensor"),
        P(None, "tensor"),
        P("dp"),
    )
    return jax.shard_map(
        shards, mesh=mesh, in_specs=placed, out_specs=P("dp", "tensor"), check_vma=False
    )
```

```python
import functools

import jax
import jax.numpy as jnp
from jax import lax
from jax.experimental import pallas as pl
from jax.experimental.pallas import tpu as pltpu
from jax.sharding import PartitionSpec as P

HEAD = 128
IMG_DEV = 4
CAP = 13
PAD = 16
TOGETHER = 6
WINDOW = 32
BLOCK_ROWS = 160
PARTS = ((0, 112), (112, 48))
GROUP_ROWS = 80
MESH = pl.DeviceIdType.MESH
F32 = jnp.float32
BF16 = jnp.bfloat16


def iota(shape, dim):
    return lax.broadcasted_iota(jnp.int32, shape, dim)


def dot(a, b, contract=((1,), (0,))):
    return lax.dot_general(a, b, (contract, ((), ())), preferred_element_type=F32)


def kernel(
    sizes,
    image_row,
    query,
    key,
    value,
    grad,
    w_query,
    w_key,
    w_value,
    out,
    rows_in,
    codes,
    position,
    send,
    recv,
    blocks,
    mask_row,
    mask_col,
    grad_mine,
    grad_send,
    grad_recv,
    weights,
    sums,
    ring_send,
    ring_recv,
    back_send,
    back_recv,
    last_send,
    last_recv,
    row_sem,
    send_sem,
    recv_sem,
    weight_sem,
    far_send_sem,
    far_recv_sem,
    grad_send_sem,
    grad_recv_sem,
    ring_send_sem,
    ring_recv_sem,
    back_send_sem,
    back_recv_sem,
    last_sem,
):
    n_dp, n_y = sizes
    tokens = query.shape[0]
    cols = query.shape[1]
    heads = cols // HEAD
    n_blocks = 4 * heads
    n_groups = n_dp // TOGETHER
    slots = n_groups * GROUP_ROWS
    half_slots = slots // 2
    chains = n_groups // 2
    upward = chains // 2
    chip_cols = out.shape[1] * 2
    me = lax.axis_index("dp")
    lane = lax.axis_index("tensor")
    core = lane % 2
    y = lane // 2
    sibling = y * 2 + (1 - core)
    above = lax.rem(y + 1, n_y) * 2 + core
    below = lax.rem(y + n_y - 1, n_y) * 2 + core

    barrier = pltpu.get_barrier_semaphore()

    def greet(step, carry):
        pl.semaphore_signal(
            barrier,
            inc=1,
            device_id=(lax.rem(me + step, n_dp), lane),
            device_id_type=MESH,
        )
        return carry

    lax.fori_loop(1, n_dp, greet, 0)
    for other in (sibling, above, below):
        pl.semaphore_signal(barrier, inc=1, device_id=(me, other), device_id_type=MESH)

    row_copies = [
        pltpu.make_async_copy(source, rows_in.at[i], row_sem.at[i])
        for i, source in enumerate((query, key, value, grad))
    ]
    for copy in row_copies:
        copy.start()

    sources = (w_query, w_key, w_value)
    weight_copies = [
        pltpu.make_async_copy(
            source, weights.at[0, :, pl.ds(i * cols, cols)], weight_sem.at[i]
        )
        for i, source in enumerate(sources)
    ]
    far_copies = [
        pltpu.make_async_remote_copy(
            src_ref=source,
            dst_ref=weights.at[1, :, pl.ds(i * cols, cols)],
            send_sem=far_send_sem.at[i],
            recv_sem=far_recv_sem.at[i],
            device_id=(me, sibling),
            device_id_type=MESH,
        )
        for i, source in enumerate(sources)
    ]

    img_r = image_row[...]
    target_r = img_r >> 2
    hit_r = jnp.where(iota((n_dp, tokens), 0) == target_r, 1.0, 0.0)
    upper = jnp.where(
        iota((tokens, tokens), 0) < iota((tokens, tokens), 1), 1.0, 0.0
    ).astype(BF16)
    before_r = dot(hit_r.astype(BF16), upper)
    pos_r = jnp.sum(before_r * hit_r, axis=0, keepdims=True)
    placed_r = target_r.astype(F32) * PAD + pos_r
    code_r = ((img_r & 3) + 1).astype(F32)
    shift = (lax.rem(me, TOGETHER) * CAP).astype(F32)
    place = jnp.where(
        iota((HEAD, tokens), 0).astype(F32) == pos_r + shift, 1.0, 0.0
    ).astype(BF16)
    last = ((1,), (1,))
    codes[...] = dot((hit_r * code_r).astype(BF16), place, last)

    tight_out = iota((BLOCK_ROWS, n_blocks * PAD), 0)
    tight_in = iota((BLOCK_ROWS, n_blocks * PAD), 1)
    tight = jnp.where(
        (tight_out == 1 + (tight_in >> 4) * CAP + (tight_in & 15)) & ((tight_in & 15) < CAP),
        1.0,
        0.0,
    ).astype(BF16)

    def message(part, place_in, target):
        rows = pl.ds(*PARTS[part])
        return pltpu.make_async_remote_copy(
            src_ref=send.at[target, rows],
            dst_ref=recv.at[place_in, rows],
            send_sem=send_sem.at[part, target],
            recv_sem=recv_sem.at[part, place_in],
            device_id=(target, lane),
            device_id_type=MESH,
        )

    def target_of(k):
        away = k // 2 + 1
        away = jnp.where(k % 2 == 0, away, n_dp - away)
        return lax.rem(me + jnp.where(k == n_dp - 1, 0, away), n_dp)

    for copy in row_copies:
        copy.wait()
    pl.semaphore_wait(barrier, n_dp + 2)

    def pack(step, carry):
        targets = [target_of(step * TOGETHER + i) for i in range(TOGETHER)]
        wanted = jnp.concatenate(
            [iota((PAD, tokens), 0) + target * PAD for target in targets], axis=0
        ).astype(F32)
        pick = jnp.where(wanted == placed_r, 1.0, 0.0).astype(BF16)
        parts = [dot(pick, ref[...]).astype(BF16) for ref in (rows_in.at[n] for n in range(4))]
        rows = []
        for head in range(heads):
            for part in parts:
                rows.append(
                    jnp.concatenate(
                        [
                            part[i * PAD : (i + 1) * PAD, head * HEAD : (head + 1) * HEAD]
                            for i in range(TOGETHER)
                        ],
                        axis=1,
                    )
                )
        packed = dot(tight, jnp.concatenate(rows, axis=0))
        code = jnp.concatenate([codes[pl.ds(target, 1), :] for target in targets], axis=1)
        packed = jnp.where(iota(packed.shape, 0) == 0, code, packed).astype(BF16)
        for i, target in enumerate(targets):
            send[target] = packed[:, i * HEAD : (i + 1) * HEAD]

            @pl.when(target != me)
            def _():
                message(0, me, target).start()

        return carry

    lax.fori_loop(0, n_groups, pack, 0)
    for copy in weight_copies + far_copies:
        copy.start()
    for part in range(1, len(PARTS)):

        def start_part(step, carry):
            message(part, me, target_of(step)).start()
            return carry

        lax.fori_loop(0, n_dp - 1, start_part, 0)
    recv[me] = send[me]
    position[...] = jnp.transpose(jnp.broadcast_to(placed_r, (HEAD, tokens)))

    def unpack(head):
        def one(which, carry):
            start = 1 + (head * 4 + which) * CAP
            top = pl.multiple_of(jnp.minimum(start // 16 * 16, BLOCK_ROWS - WINDOW), 16)
            skip = start - top
            shape = (GROUP_ROWS, TOGETHER * WINDOW)
            to, source = iota(shape, 0), iota(shape, 1)
            within = (source & (WINDOW - 1)) - skip
            loose = jnp.where(
                (to == (source >> 5) * CAP + within) & (within >= 0) & (within < CAP),
                1.0,
                0.0,
            ).astype(BF16)
            wide = jnp.concatenate(
                [
                    jnp.concatenate(
                        [
                            recv[g * TOGETHER + i, pl.ds(top, WINDOW), :]
                            for g in range(n_groups)
                        ],
                        axis=1,
                    )
                    for i in range(TOGETHER)
                ],
                axis=0,
            )
            spread = dot(loose, wide).astype(BF16)
            for g in range(n_groups):
                blocks[which, g * GROUP_ROWS : (g + 1) * GROUP_ROWS, :] = spread[
                    :, g * HEAD : (g + 1) * HEAD
                ]
            return carry

        lax.fori_loop(0, 4, one, 0)

    def codes_in():
        total = None
        for g in range(n_groups):
            tile = recv[g * TOGETHER, :16, :].astype(F32)
            for i in range(1, TOGETHER):
                tile = tile + recv[g * TOGETHER + i, :16, :].astype(F32)
            only = jnp.where(iota((16, HEAD), 0) == 0, tile, 0.0).astype(BF16)
            shape = (HEAD, slots)
            there = iota(shape, 0)
            put = jnp.where(
                (iota(shape, 1) == g * GROUP_ROWS + there) & (there < GROUP_ROWS), 1.0, 0.0
            ).astype(BF16)
            term = dot(only, put)
            total = term if total is None else total + term
        code_row = jnp.sum(total, axis=0, keepdims=True)
        mask_row[...] = code_row
        mask_col[...] = jnp.transpose(jnp.broadcast_to(code_row, (HEAD, slots)))

    scale = HEAD ** (-0.5)

    def to_sibling(head):
        return pltpu.make_async_remote_copy(
            src_ref=grad_send.at[head],
            dst_ref=grad_recv.at[head],
            send_sem=grad_send_sem.at[head],
            recv_sem=grad_recv_sem.at[head],
            device_id=(me, sibling),
            device_id_type=MESH,
        )

    def attend(head):
        q = blocks[0]
        k = blocks[1]
        v = blocks[2]
        g = blocks[3]
        allowed = mask_col[:, 0:1] == mask_row[...]
        scores = jnp.where(allowed, dot(k, q, last), -1e30)
        highest = jnp.max(scores, axis=0, keepdims=True)
        raised = jnp.exp((scores - highest) * scale)
        attention = raised * (1.0 / jnp.sum(raised, axis=0, keepdims=True))
        grad_prob = dot(v, g, last)
        row_total = jnp.sum(attention * grad_prob, axis=0, keepdims=True)
        dscore = (attention * (grad_prob - row_total) * scale).astype(BF16)
        grad_value = dot(attention.astype(BF16), g).astype(BF16)
        grad_key = dot(dscore, q).astype(BF16)
        grad_query = jnp.transpose(dot(k, dscore, ((0,), (0,)))).astype(BF16)
        first = core == 0
        for i, result in enumerate((grad_query, grad_key, grad_value)):
            low, high = result[:half_slots], result[half_slots:]
            left = slice(i * HEAD, (i + 1) * HEAD)
            grad_mine[head, :, left] = jnp.where(first, low, high)
            grad_send[head, :, left] = jnp.where(first, high, low)
        to_sibling(head).start()

    def chunk_of(o):
        ahead = (n_y - o) // 2
        return lax.rem(y + n_y + jnp.where(o % 2 == 1, -ahead, ahead), n_y)

    def product(source, owner, o, some):
        left = pl.multiple_of(chunk_of(o) * chip_cols, chip_cols)
        rows = jnp.concatenate([source[head] for head in some], axis=1)
        w = jnp.concatenate(
            [
                weights[
                    owner,
                    pl.ds(left, chip_cols),
                    i * cols + head * HEAD : i * cols + (head + 1) * HEAD,
                ]
                for head in some
                for i in range(3)
            ],
            axis=1,
        )
        return dot(rows, w, last)

    def project_first(o, carry):
        early = range(heads - 1)
        sums[o] = product(grad_mine, 0, o, early) + product(grad_recv, 1, o, early)
        return carry

    def project_last(o, carry):
        some = (heads - 1,)
        sums[o] += product(grad_mine, 0, o, some) + product(grad_recv, 1, o, some)
        return carry

    def left_part(part):
        def left_one(step, carry):
            other = lax.rem(me + step, n_dp)
            message(part, other, other).wait_send()
            return carry

        lax.fori_loop(1, n_dp, left_one, 0)

    def one_head(head, carry):
        for part in range(len(PARTS)):

            @pl.when(head == part * (heads - 1))
            def _():
                def wait_part(step, carry):
                    other = lax.rem(me + step, n_dp)
                    message(part, other, other).wait_recv()
                    return carry

                lax.fori_loop(1, n_dp, wait_part, 0)

        unpack(head)
        pl.when(head == 0)(codes_in)
        attend(head)

        @pl.when(head == heads - 2)
        def _():
            for copy in weight_copies:
                copy.wait()
            for copy in far_copies:
                copy.wait_recv()
            for early in range(heads - 1):
                to_sibling(early).wait_recv()
            lax.fori_loop(0, n_y, project_first, 0)
            for part in range(len(PARTS) - 1):
                left_part(part)
            for copy in far_copies:
                copy.wait_send()

        return carry

    lax.fori_loop(0, heads, one_head, 0)

    reach = n_y // 2
    first_set = range(upward)
    second_set = range(upward, chains)

    def hop(way, step, chain):
        slot = (way * reach + step) * chains + chain
        return pltpu.make_async_remote_copy(
            src_ref=ring_send.at[slot],
            dst_ref=ring_recv.at[slot],
            send_sem=ring_send_sem.at[slot],
            recv_sem=ring_recv_sem.at[slot],
            device_id=(me, above if way else below),
            device_id_type=MESH,
        )

    def rows_of(o, chain):
        return sums[o, chain * GROUP_ROWS : (chain + 1) * GROUP_ROWS, :]

    def arrived(way, step, chain):
        hop(way, step, chain).wait_recv()
        return ring_recv[(way * reach + step) * chains + chain].astype(F32)

    def first_hop(way, chain, o):
        ring_send[way * reach * chains + chain] = rows_of(o, chain).astype(BF16)
        hop(way, 0, chain).start()

    def next_hop(way, step, chain, o):
        slot = (way * reach + step) * chains + chain
        ring_send[slot] = (rows_of(o, chain) + arrived(way, step - 1, chain)).astype(BF16)
        hop(way, step, chain).start()

    to_sibling(heads - 1).wait_recv()
    project_last(0, 0)
    for down, up in zip(first_set, second_set):
        first_hop(0, down, 0)
        first_hop(1, up, 0)
    lax.fori_loop(1, 3, project_last, 0)
    for down, up in zip(second_set, first_set):
        first_hop(0, down, 1)
        first_hop(1, up, 2)

    def ring_step(step, carry):
        for down, up in zip(first_set, second_set):
            next_hop(0, step, down, 2 * step - 1)
            next_hop(1, step, up, 2 * step)
        lax.fori_loop(2 * step + 1, jnp.minimum(2 * step + 3, n_y), project_last, 0)

        @pl.when(step < reach - 1)
        def _():
            for down, up in zip(second_set, first_set):
                next_hop(0, step, down, 2 * step + 1)
                next_hop(1, step, up, 2 * step + 2)

        return carry

    lax.fori_loop(1, reach, ring_step, 0)

    def back(index, target, home):
        return pltpu.make_async_remote_copy(
            src_ref=back_send.at[index],
            dst_ref=back_recv.at[home],
            send_sem=back_send_sem.at[index],
            recv_sem=back_recv_sem.at[home],
            device_id=(target, lane),
            device_id_type=MESH,
        )

    shape = (TOGETHER * PAD, GROUP_ROWS)
    to, source = iota(shape, 0), iota(shape, 1)
    apart = jnp.where(
        (source == (to >> 4) * CAP + (to & 15)) & ((to & 15) < CAP), 1.0, 0.0
    ).astype(BF16)
    for pair in range(upward):
        for chain in (pair, upward + pair):
            longer = 0 if chain in first_set else 1
            final = rows_of(n_y - 1, chain) + arrived(1 - longer, reach - 2, chain)
            final = (final + arrived(longer, reach - 1, chain)).astype(BF16)
            laid = dot(apart, final).astype(BF16)
            for i in range(TOGETHER):
                index = chain * TOGETHER + i
                target = (core * chains + chain) * TOGETHER + i
                back_send[index] = laid[i * PAD : (i + 1) * PAD]

                @pl.when(target != me)
                def _():
                    back(index, target, me).start()

                @pl.when(target == me)
                def _():
                    back_recv[me] = back_send[index]

    half_dp = n_dp // 2
    mine = (me // half_dp) == core

    def to_last():
        return pltpu.make_async_remote_copy(
            src_ref=last_send,
            dst_ref=last_recv,
            send_sem=last_sem.at[0],
            recv_sem=last_sem.at[1],
            device_id=(me, sibling),
            device_id_type=MESH,
        )

    def drain():
        left_part(len(PARTS) - 1)
        for head in range(heads):
            to_sibling(head).wait_send()

        def left_hop(step, carry):
            for chain in range(chains):
                hop(0, step, chain).wait_send()
                hop(1, step, chain).wait_send()
            return carry

        lax.fori_loop(0, reach - 1, left_hop, 0)
        for down, up in zip(first_set, second_set):
            hop(0, reach - 1, down).wait_send()
            hop(1, reach - 1, up).wait_send()

        def left_back(index, carry):
            target = core * half_dp + index

            @pl.when(target != me)
            def _():
                back(index, target, me).wait_send()

            return carry

        lax.fori_loop(0, half_dp, left_back, 0)

    @pl.when(mine)
    def _():
        width = out.shape[1]
        wide = last_send.shape[1]
        pick = jnp.where(
            iota((tokens, n_dp * PAD), 1).astype(F32) == position[:, 0:1], 1.0, 0.0
        ).astype(BF16)
        def wait_back(step, carry):
            home = lax.rem(me + step, n_dp)
            back(0, home, home).wait_recv()
            return carry

        lax.fori_loop(1, n_dp, wait_back, 0)
        every = back_recv[...].reshape(n_dp * PAD, chip_cols)
        rows = dot(pick, every)

        @pl.when(core == 0)
        def _():
            last_send[...] = rows[:, chip_cols - wide :].astype(BF16)
            to_last().start()
            out[...] = rows[:, :width].astype(BF16)

        @pl.when(core == 1)
        def _():
            last_send[...] = rows[:, :wide].astype(BF16)
            to_last().start()
            out[...] = rows[:, width:].astype(BF16)

        drain()
        to_last().wait_send()

    @pl.when(jnp.logical_not(mine))
    def _():
        width = out.shape[1]
        wide = last_recv.shape[1]
        drain()
        to_last().wait_recv()

        @pl.when(core == 0)
        def _():
            out[...] = last_recv[:, :width]

        @pl.when(core == 1)
        def _():
            out[...] = last_recv[:, wide - width :]


def shards(query_rows, key_rows, value_rows, out_grad, w_query, w_key, w_value, row_image):
    n_dp = lax.axis_size("dp")
    n_tensor = lax.axis_size("tensor")
    n_y = n_tensor // 2
    tokens, cols = query_rows.shape
    features = w_query.shape[0]
    width = features // n_tensor
    chip_cols = 2 * width
    wide = (width + HEAD - 1) // HEAD * HEAD
    heads = cols // HEAD
    n_groups = n_dp // TOGETHER
    slots = n_groups * GROUP_ROWS
    chains = n_groups // 2
    hops = n_y * chains
    vmem = pl.BlockSpec(memory_space=pltpu.VMEM)
    hbm = pl.BlockSpec(memory_space=pl.ANY)
    dma = pltpu.SemaphoreType.DMA
    return pl.pallas_call(
        functools.partial(kernel, (n_dp, n_y)),
        out_shape=jax.ShapeDtypeStruct((tokens, width), BF16),
        in_specs=[vmem] + [hbm] * 7,
        out_specs=vmem,
        scratch_shapes=[
            pltpu.VMEM((4, tokens, cols), BF16),
            pltpu.VMEM((n_dp, HEAD), F32),
            pltpu.VMEM((tokens, HEAD), F32),
            pltpu.VMEM((n_dp, BLOCK_ROWS, HEAD), BF16),
            pltpu.VMEM((n_dp, BLOCK_ROWS, HEAD), BF16),
            pltpu.VMEM((4, slots, HEAD), BF16),
            pltpu.VMEM((1, slots), F32),
            pltpu.VMEM((slots, HEAD), F32),
            pltpu.VMEM((heads, slots // 2, 3 * HEAD), BF16),
            pltpu.VMEM((heads, slots // 2, 3 * HEAD), BF16),
            pltpu.VMEM((heads, slots // 2, 3 * HEAD), BF16),
            pltpu.VMEM((2, features, 3 * cols), BF16),
            pltpu.VMEM((n_y, slots // 2, chip_cols), F32),
            pltpu.VMEM((hops, GROUP_ROWS, chip_cols), BF16),
            pltpu.VMEM((hops, GROUP_ROWS, chip_cols), BF16),
            pltpu.VMEM((n_dp // 2, PAD, chip_cols), BF16),
            pltpu.VMEM((n_dp, PAD, chip_cols), BF16),
            pltpu.VMEM((tokens, wide), BF16),
            pltpu.VMEM((tokens, wide), BF16),
            dma((4,)),
            dma((len(PARTS), n_dp)),
            dma((len(PARTS), n_dp)),
            dma((3,)),
            dma((3,)),
            dma((3,)),
            dma((heads,)),
            dma((heads,)),
            dma((hops,)),
            dma((hops,)),
            dma((n_dp // 2,)),
            dma((n_dp,)),
            dma((2,)),
        ],
        compiler_params=pltpu.CompilerParams(
            collective_id=0, has_side_effects=True, vmem_limit_bytes=56 * 2**20
        ),
    )(
        row_image.reshape(1, tokens),
        query_rows,
        key_rows,
        value_rows,
        out_grad,
        w_query,
        w_key,
        w_value,
    )


def solution(mesh):
    placed = (
        P("dp", "tensor"),
        P("dp", "tensor"),
        P("dp", "tensor"),
        P("dp", "tensor"),
        P(None, "tensor"),
        P(None, "tensor"),
        P(None, "tensor"),
        P("dp"),
    )
    return jax.shard_map(
        shards, mesh=mesh, in_specs=placed, out_specs=P("dp", "tensor"), check_vma=False
    )
```
